32 devices in a mesh: blk: 8 (over z, x), tok: 4 (over y, core).
Axes of the slice: x: 2, y: 2, z: 4, core: 2. Of those that a mesh axis runs over, the one named last changes fastest.
Arguments:
- acts: bfloat16 [1024, 2, 14336], P('tok', None, 'blk'), may hold values from -6 to 6
Outputs:
- hessian: bfloat16 [2, 14336, 28672], P(None, ('blk', 'tok'))
The draws below stay inside these ranges and needn't reach their ends.
All inputs are finite; a program needn't handle non-finite values.
Results may differ from the reference program's by a relative error of at most 0.0085.
Values may be sent and summed in bfloat16 or wider, within the bound.
No kernel may reach another device: no remote copies, remote signals or barrier semaphores. Data moves between devices by JAX's collectives and lax.ppermute only.
A program may use at most 384 MiB of HBM per device.

```python
import jax
import jax.numpy as jnp
from jax import lax

F = 28672
TOK_DEV = 256
TOKENS = 1024
BLOCKS = 16
ROWS = 1792
HALF = 14336


def levels(stream_key, shape, cuts, least, top_value):
    loudness, own = 1.0, jax.random.fold_in(stream_key, 6)
    for axis_at, blocks in cuts:
        heights = jnp.exp(jax.random.uniform(jax.random.fold_in(own, axis_at), (blocks,), jnp.float32, least / len(cuts), top_value / len(cuts)))
        loudness = loudness * jnp.repeat(heights, shape[axis_at] // blocks).reshape([-1 if axis == axis_at else 1 for axis in range(len(shape))])
    return loudness


def noise(key, extent, scale, most, split=(), held_as=jnp.bfloat16):
    loudness = levels(key, extent, split, -0.22, 0.18) if split else 1.0
    result = jax.random.normal(key, extent, jnp.float32) * scale * loudness
    return jnp.minimum(jnp.maximum(result, -most), most).astype(held_as)


def setup_inputs(seed: int = 0) -> dict:
    splits = jax.random.split(jax.random.key(seed), 2)
    return {
        "acts": noise(splits[0], (TOKENS, 2, HALF), 1.0, 6.0, ((0, 4), (2, 8))),
    }


def reference(acts):
    back = acts[:, 1, :].reshape(TOKENS, BLOCKS // 2, ROWS)[:, ::-1, :].reshape(TOKENS, HALF)
    matrix = jnp.concatenate([acts[:, 0, :], back], axis=1)
    groups = matrix.reshape(TOKENS // TOK_DEV, TOK_DEV, F)
    order = jnp.concatenate([jnp.arange(BLOCKS // 2, dtype=jnp.int32), BLOCKS - 1 - jnp.arange(BLOCKS // 2, dtype=jnp.int32)])

    def row_block(block):
        start = (block * ROWS).astype(jnp.int32)
        total = jnp.zeros((ROWS, F), jnp.float32)
        for group in range(TOKENS // TOK_DEV):
            members = groups[group]
            chosen = lax.dynamic_slice_in_dim(members, start, ROWS, 1)
            partial_sum = jnp.dot(chosen.T, members, preferred_element_type=jnp.float32)
            rounded = lax.optimization_barrier(partial_sum.astype(jnp.bfloat16))
            total = total + rounded.astype(jnp.float32)
        return (total * (2.0 / TOKENS)).astype(jnp.bfloat16)

    blocks = lax.map(row_block, order)
    return blocks.reshape(2, HALF, F)
```

```python
import functools

import jax
import jax.numpy as jnp
from jax import lax
from jax.experimental import pallas as pl
from jax.experimental.pallas import tpu as pltpu
from jax.sharding import PartitionSpec as P

LANES = 128
CSPLIT = 2
VMEM = 24 * 2**20


def left_kernel(count, tok_ref, *refs):
    out_ref = refs[-1]
    strip = out_ref.shape[1]
    rows = refs[0].shape[-1]
    row = lax.broadcasted_iota(jnp.int32, (strip, rows), 0)
    col = lax.broadcasted_iota(jnp.int32, (strip, rows), 1)
    pick = jnp.where(col == row + tok_ref[0] * strip, 1.0, 0.0).astype(jnp.bfloat16)
    for h in range(2):
        at = 0
        for ref in refs[h * count : (h + 1) * count]:
            part = lax.dot_general(
                pick, ref[...], (((1,), (1,)), ((), ())), preferred_element_type=jnp.float32
            )
            out_ref[h, :, at : at + ref.shape[0]] = part.astype(out_ref.dtype)
            at += ref.shape[0]


def operand(pair, block, index):
    array, at = pair
    if at is None:
        return array, pl.BlockSpec(block, index)
    return array, pl.BlockSpec((None, *block), lambda *i: (at, *index(*i)))


def left_rows(tok, pairs, strip):
    rows = pairs[0][0].shape[-1]
    given = [operand(p, p[0].shape[-2:], lambda i, t: (0, 0)) for p in pairs]
    depth = sum(p[0].shape[-2] for p in pairs) // 2
    shape = (2, strip, depth)
    return pl.pallas_call(
        functools.partial(left_kernel, len(pairs) // 2),
        out_shape=jax.ShapeDtypeStruct(shape, jnp.bfloat16),
        grid_spec=pltpu.PrefetchScalarGridSpec(
            num_scalar_prefetch=1,
            grid=(1,),
            in_specs=[g[1] for g in given],
            out_specs=pl.BlockSpec(shape, lambda i, t: (0, 0, 0)),
        ),
        compiler_params=pltpu.CompilerParams(vmem_limit_bytes=VMEM),
        cost_estimate=pl.CostEstimate(
            flops=2 * 2 * strip * depth * rows,
            bytes_accessed=2 * 2 * depth * rows,
            transcendentals=0,
        ),
    )(tok[None], *[g[0] for g in given])


def column_kernel(factor, parts, cols_ref, left_ref, *rest):
    out_ref = rest[-1]
    right = jnp.concatenate([r[...] for r in rest[:parts]], axis=0)
    part = jnp.dot(left_ref[...], right, preferred_element_type=jnp.float32)
    out_ref[...] = (part * factor).astype(out_ref.dtype)


def column_block(out, left, pairs, cols, which, width, factor):
    block = pairs[0][0].shape[-1]
    halves, strip, depth = left.shape
    given = [operand(p, p[0].shape[-2:], lambda i, c: (0, 0)) for p in pairs]
    in_specs = [pl.BlockSpec((None, strip, depth), lambda i, c: (i, 0, 0))]
    in_specs += [g[1] for g in given]
    operands = [cols, left] + [g[0] for g in given]
    aliases = {}
    if out is not None:
        in_specs.append(pl.BlockSpec(memory_space=pl.ANY))
        aliases = {len(operands): 0}
        operands.append(out)
    return pl.pallas_call(
        functools.partial(column_kernel, factor, len(pairs)),
        out_shape=jax.ShapeDtypeStruct((2, strip, width), jnp.bfloat16),
        grid_spec=pltpu.PrefetchScalarGridSpec(
            num_scalar_prefetch=1,
            grid=(halves,),
            in_specs=in_specs,
            out_specs=pl.BlockSpec((None, strip, block), lambda i, c: (i, 0, c[which])),
        ),
        input_output_aliases=aliases,
        compiler_params=pltpu.CompilerParams(vmem_limit_bytes=VMEM),
        cost_estimate=pl.CostEstimate(
            flops=2 * 2 * strip * depth * block,
            bytes_accessed=2 * (depth * (block + 2 * strip) + 2 * strip * block),
            transcendentals=0,
        ),
    )(*operands)


def gathered(acts):
    nblk, ntok = lax.axis_size("blk"), lax.axis_size("tok")
    tok_rows, _, rows = acts.shape
    strip = rows // ntok
    tok = lax.axis_index("tok")
    halves = jnp.swapaxes(acts, 0, 1)
    group = lax.all_gather(halves, "tok", axis=0)
    left = lax.dynamic_slice_in_dim(group, tok * strip, strip, 3)
    whole = lax.all_gather(group, "blk", axis=0)
    order = jnp.concatenate([whole[:, :, 0], whole[::-1, :, 1]], axis=0)
    product = jnp.einsum("thks,ctkr->hscr", left, order, preferred_element_type=jnp.float32)
    scaled = (product * (2.0 / (tok_rows * ntok))).astype(jnp.bfloat16)
    return scaled.reshape(2, strip, 2 * nblk * rows)


STEPS = [
    (("S", 1, 0), ("X", 0, 1), ("Y", 0, 0)),
    (("S", 1, 1), ("X", 0, 0), ("Y", 0, 1)),
    (("S", 2, 0), ("D", 0, 0), ("D", 0, 1)),
    (("S", 2, 1), ("X", 1, 0), ("Y", 1, 0)),
    (("S", 3, 0), ("X", 1, 1), ("Y", 1, 1)),
    (("S", 3, 1), ("X", 2, 0), ("Y", 2, 0)),
    (("D", 1, 0), ("X", 2, 1), ("Y", 2, 1)),
    (("D", 1, 1), ("X", 3, 1), ("Y", 3, 0)),
    (("D", 2, 0), ("X", 3, 0), ("Y", 3, 1)),
    (("D", 2, 1), ("D", 3, 0), ("D", 3, 1)),
]


def source(link, name):
    place, k, h = name
    if link == 0:
        return place, k - 1, h
    if place == "D":
        return ("Y" if link == 1 else "X"), k, h
    return "S", k, h


def meshed(acts):
    nblk, ntok = lax.axis_size("blk"), lax.axis_size("tok")
    nz = nblk // 2
    tok_rows, _, rows = acts.shape
    strip = rows // ntok
    width = 2 * nblk * rows
    factor = 2.0 / (tok_rows * ntok)
    axes = ("blk", "tok")
    places = [
        (z, x, y, c)
        for z in range(nz)
        for x in range(2)
        for y in range(2)
        for c in range(2)
    ]

    def at(z, x, y, c):
        return ((z * 2 + x) * 2 + y) * 2 + c

    links = [
        [(at(z, x, y, c), at((z + 1) % nz, x, y, c)) for z, x, y, c in places],
        [(at(z, x, y, c), at(z, 1 - x, y, c)) for z, x, y, c in places],
        [(at(z, x, y, c), at(z, x, 1 - y, c)) for z, x, y, c in places],
    ]
    cores = [(at(z, x, y, c), at(z, x, y, 1 - c)) for z, x, y, c in places]

    blk, tok = lax.axis_index("blk"), lax.axis_index("tok")
    z, x = blk // 2, blk % 2
    cols = []
    for k in range(nz):
        zk = (z - k) % nz
        for xk in (x, 1 - x):
            cols += [2 * zk + xk, 2 * nblk - 1 - (2 * zk + xk)]
    cols = jnp.stack(cols).astype(jnp.int32)

    mine = {("S", 0, 0): acts[:, 0, :], ("S", 0, 1): acts[:, 1, :]}
    other = {}
    ready = {("S", 0, 0): 0, ("S", 0, 1): 0}

    def swap(a):
        cut = a.shape[0] // CSPLIT
        return [lax.ppermute(a[i * cut : (i + 1) * cut], axes, cores) for i in range(CSPLIT)]

    for h in range(2):
        other["S", 0, h] = swap(mine["S", 0, h])

    out, left = None, None
    pending = {}
    for i, step in enumerate(STEPS):
        for name in step:
            ready[name] = i + 1
    todo = []
    for k in range(nz):
        for xi, (near, far) in enumerate((("S", "Y"), ("X", "D"))):
            for h in range(2):
                todo.append((max(ready[near, k, h], ready[far, k, h]), (near, k, h), (far, k, h), (2 * k + xi) * 2 + h))
    todo.sort()

    def start(i):
        for link, name in enumerate(STEPS[i]):
            pending[name] = lax.ppermute(mine[source(link, name)], axes, links[link])

    def pairs_of(near, far):
        return [(a, None) for a in (mine[near], *other[near], mine[far], *other[far])]

    def compute(upto):
        nonlocal out, left
        if left is None:
            left = left_rows(
                tok,
                [p for h in range(2) for p in pairs_of(("S", 0, h), ("Y", 0, h))],
                strip,
            )
        while todo and todo[0][0] <= upto:
            _, near, far, which = todo.pop(0)
            out = column_block(out, left, pairs_of(near, far), cols, which, width, factor)

    start(0)
    start(1)
    for i, step in enumerate(STEPS):
        arrived = [pending.pop(name) for name in step]
        *arrived, cols = lax.optimization_barrier((*arrived, cols))
        mine.update(zip(step, arrived))
        other.update((name, swap(mine[name])) for name in step)
        if i >= 2:
            compute(i)
        if i + 2 < len(STEPS):
            names = sorted({source(link, name) for link, name in enumerate(STEPS[i + 2])})
            held = ([mine[n] for n in names], [other[n] for n in step], cols)
            if out is None:
                held, swapped, cols = lax.optimization_barrier(held)
            else:
                held, swapped, cols, out = lax.optimization_barrier((*held, out))
            mine.update(zip(names, held))
            other.update(zip(step, swapped))
            start(i + 2)
    compute(len(STEPS))
    return out


def local(acts):
    if lax.axis_size("blk") == 8 and lax.axis_size("tok") == 4 and acts.shape[2] % LANES == 0:
        return meshed(acts)
    return gathered(acts)


def solution(mesh):
    return jax.shard_map(
        local,
        mesh=mesh,
        in_specs=(P("tok", None, "blk"),),
        out_specs=P(None, ("blk", "tok"), None),
        check_vma=False,
    )
```

```python
import functools

import jax
import jax.numpy as jnp
from jax import lax
from jax.experimental import pallas as pl
from jax.experimental.pallas import tpu as pltpu
from jax.sharding import PartitionSpec as P

LANES = 128
KSCALE = 1
CALLS = (2, 3, 5, 6, 7, 8, 9, 10)
VMEM = 56 * 2**20


def picked(ref, at):
    return ref if at is None else ref.at[at]


def left_kernel(count, picks, tok_ref, *refs):
    parts, out_ref, held, sems = refs[: 2 * count], refs[-3], refs[-2], refs[-1]
    strip = out_ref.shape[1]
    window = held.shape[2]
    first = tok_ref[0] * strip
    base = pl.multiple_of(first // LANES * LANES, LANES)
    copies = []
    for h in range(2):
        at = 0
        for i, ref in enumerate(parts[h * count : (h + 1) * count]):
            depth = ref.shape[-2]
            copies.append(
                pltpu.make_async_copy(
                    picked(ref, picks[h * count + i]).at[:, pl.ds(base, window)], held.at[h, at : at + depth], sems.at[h, i]
                )
            )
            at += depth
    for copy in copies:
        copy.start()
    row = lax.broadcasted_iota(jnp.int32, (strip, window), 0)
    col = lax.broadcasted_iota(jnp.int32, (strip, window), 1)
    pick = jnp.where(col == row + (first - base), 1.0, 0.0).astype(jnp.bfloat16)
    for copy in copies:
        copy.wait()
    for h in range(2):
        part = lax.dot_general(
            pick, held[h], (((1,), (1,)), ((), ())), preferred_element_type=jnp.float32
        )
        out_ref[h] = part.astype(out_ref.dtype)


def left_rows(tok, parts, strip):
    picks = [p[1] for p in parts]
    parts = [p[0] for p in parts]
    depth = sum(p.shape[-2] for p in parts) // 2
    shape = (2, strip, depth)
    window = (strip + LANES // 2 + LANES - 1) // LANES * LANES
    return pl.pallas_call(
        functools.partial(left_kernel, len(parts) // 2, picks),
        out_shape=jax.ShapeDtypeStruct(shape, jnp.bfloat16),
        in_specs=[pl.BlockSpec(memory_space=pltpu.SMEM)]
        + [pl.BlockSpec(memory_space=pl.ANY)] * len(parts),
        out_specs=pl.BlockSpec(memory_space=pltpu.VMEM),
        scratch_shapes=[
            pltpu.VMEM((2, depth, window), jnp.bfloat16),
            pltpu.SemaphoreType.DMA((2, len(parts) // 2)),
        ],
        compiler_params=pltpu.CompilerParams(vmem_limit_bytes=VMEM),
        cost_estimate=pl.CostEstimate(
            flops=2 * 2 * strip * depth * window,
            bytes_accessed=2 * 2 * depth * (window + strip),
            transcendentals=0,
        ),
    )(tok[None], *parts)


def column_kernel(factor, parts, picks, cols_ref, left_ref, *refs):
    blocks = len(parts)
    count = sum(len(p) for p in parts)
    rights, out_ref, held, sems = refs[:count], refs[-3], refs[-2], refs[-1]
    block, half = pl.program_id(0), pl.program_id(1)
    last = pl.num_programs(1) - 1

    def copies(b):
        first = sum(len(p) for p in parts[:b])
        at, found = 0, []
        for i, depth in enumerate(parts[b]):
            found.append(
                pltpu.make_async_copy(
                    picked(rights[first + i], picks[b][i]),
                    held.at[b % 2, at : at + depth],
                    sems.at[b % 2, i],
                )
            )
            at += depth
        return found

    @pl.when((block == 0) & (half == 0))
    def _():
        for b in range(min(2, blocks)):
            for copy in copies(b):
                copy.start()

    for b in range(blocks):

        @pl.when((block == b) & (half == 0))
        def _(b=b):
            for copy in copies(b):
                copy.wait()

    part = jnp.dot(left_ref[...], held[block % 2], preferred_element_type=jnp.float32)
    out_ref[...] = (part * factor).astype(out_ref.dtype)
    for b in range(blocks - 2):

        @pl.when((block == b) & (half == last))
        def _(b=b):
            for copy in copies(b + 2):
                copy.start()


def column_blocks(out, left, groups, cols, width, factor):
    block = groups[0][0][0].shape[-1]
    halves, strip, depth = left.shape
    parts = [[a.shape[-2] for a, _ in g] for g in groups]
    picks = [[at for _, at in g] for g in groups]
    anywhere = pl.BlockSpec(memory_space=pl.ANY)
    operands = [cols, left] + [a for g in groups for a, _ in g]
    in_specs = [pl.BlockSpec((None, strip, depth), lambda b, i, c: (i, 0, 0))]
    in_specs += [anywhere] * (len(operands) - 2)
    aliases = {}
    if out is not None:
        in_specs.append(anywhere)
        aliases = {len(operands): 0}
        operands.append(out)
    return pl.pallas_call(
        functools.partial(column_kernel, factor, parts, picks),
        out_shape=jax.ShapeDtypeStruct((2, strip, width), jnp.bfloat16),
        grid_spec=pltpu.PrefetchScalarGridSpec(
            num_scalar_prefetch=1,
            grid=(len(groups), halves),
            in_specs=in_specs,
            out_specs=pl.BlockSpec((None, strip, block), lambda b, i, c: (i, 0, c[b])),
            scratch_shapes=[
                pltpu.VMEM((min(2, len(groups)), depth, block), jnp.bfloat16),
                pltpu.SemaphoreType.DMA((2, max(len(p) for p in parts))),
            ],
        ),
        input_output_aliases=aliases,
        compiler_params=pltpu.CompilerParams(vmem_limit_bytes=VMEM),
        cost_estimate=pl.CostEstimate(
            flops=int(KSCALE * 2 * 2 * strip * depth * block * len(groups)),
            bytes_accessed=2 * (depth * (block + 2 * strip) + 2 * strip * block) * len(groups),
            transcendentals=0,
        ),
    )(*operands)


def gathered(acts):
    nblk, ntok = lax.axis_size("blk"), lax.axis_size("tok")
    tok_rows, _, rows = acts.shape
    strip = rows // ntok
    tok = lax.axis_index("tok")
    halves = jnp.swapaxes(acts, 0, 1)
    group = lax.all_gather(halves, "tok", axis=0)
    left = lax.dynamic_slice_in_dim(group, tok * strip, strip, 3)
    whole = lax.all_gather(group, "blk", axis=0)
    order = jnp.concatenate([whole[:, :, 0], whole[::-1, :, 1]], axis=0)
    product = jnp.einsum("thks,ctkr->hscr", left, order, preferred_element_type=jnp.float32)
    scaled = (product * (2.0 / (tok_rows * ntok))).astype(jnp.bfloat16)
    return scaled.reshape(2, strip, 2 * nblk * rows)


STEPS = [
    (("S", 1, 0), ("X", 0, 1), ("Y", 0, 0)),
    (("S", 1, 1), ("X", 0, 0), ("Y", 0, 1)),
    (("S", 2, 0), ("D", 0, 0), ("D", 0, 1)),
    (("S", 2, 1), ("X", 1, 0), ("Y", 1, 0)),
    (("S", 3, 0), ("X", 1, 1), ("Y", 1, 1)),
    (("S", 3, 1), ("X", 2, 0), ("Y", 2, 0)),
    (("D", 1, 0), ("X", 2, 1), ("Y", 2, 1)),
    (("D", 1, 1), ("X", 3, 1), ("Y", 3, 0)),
    (("D", 2, 0), ("X", 3, 0), ("Y", 3, 1)),
    (("D", 2, 1), ("D", 3, 0), ("D", 3, 1)),
]


def source(link, name):
    place, k, h = name
    if link == 0:
        return place, k - 1, h
    if place == "D":
        return ("Y" if link == 1 else "X"), k, h
    return "S", k, h


def meshed(acts):
    nblk, ntok = lax.axis_size("blk"), lax.axis_size("tok")
    nz = nblk // 2
    tok_rows, _, rows = acts.shape
    strip = rows // ntok
    width = 2 * nblk * rows
    factor = 2.0 / (tok_rows * ntok)
    axes = ("blk", "tok")
    places = [
        (z, x, y, c)
        for z in range(nz)
        for x in range(2)
        for y in range(2)
        for c in range(2)
    ]

    def at(z, x, y, c):
        return ((z * 2 + x) * 2 + y) * 2 + c

    links = [
        [(at(z, x, y, c), at((z + 1) % nz, x, y, c)) for z, x, y, c in places],
        [(at(z, x, y, c), at(z, 1 - x, y, c)) for z, x, y, c in places],
        [(at(z, x, y, c), at(z, x, 1 - y, c)) for z, x, y, c in places],
    ]
    cores = [(at(z, x, y, c), at(z, x, y, 1 - c)) for z, x, y, c in places]

    blk, tok = lax.axis_index("blk"), lax.axis_index("tok")
    z, x = blk // 2, blk % 2
    cols = []
    for k in range(nz):
        zk = (z - k) % nz
        for xk in (x, 1 - x):
            cols += [2 * zk + xk, 2 * nblk - 1 - (2 * zk + xk)]
    cols = [c.astype(jnp.int32) for c in cols]

    own = lax.optimization_barrier((acts[:, 0, :], acts[:, 1, :]))
    mine = {("S", 0, 0): own[0], ("S", 0, 1): own[1]}
    other = {}
    ready = {("S", 0, 0): 0, ("S", 0, 1): 0}

    out, left = None, None
    pending = {}
    for i, step in enumerate(STEPS):
        for name in step:
            ready[name] = i + 1
    todo = []
    for k in range(nz):
        for xi, (near, far) in enumerate((("S", "Y"), ("X", "D"))):
            for h in range(2):
                todo.append((max(ready[near, k, h], ready[far, k, h]), (near, k, h), (far, k, h), (2 * k + xi) * 2 + h))
    todo.sort()
    calls, first = [], 0
    for upto in CALLS:
        end = sum(t[0] <= upto for t in todo)
        ends = [first + 1, end] if upto + 1 == len(STEPS) else [end]
        for stop in ends:
            calls.append([t[3] for t in todo[first:stop]])
            first = stop
    cols = [jnp.stack([cols[w] for w in call]) for call in calls]

    def start(i):
        for link, name in enumerate(STEPS[i]):
            pending[name] = lax.ppermute(mine[source(link, name)], axes, links[link])

    def parts_of(near, far):
        return [(mine[near], None), other[near], (mine[far], None), other[far]]

    def due(upto):
        now = [t for t in todo if t[0] <= upto]
        del todo[: len(now)]
        return [parts_of(near, far) for _, near, far, _ in now]

    def swap(given, groups, out):
        arrays = [[a for a, _ in g] for g in groups]
        picks = [[at for _, at in g] for g in groups]

        def run(given, arrays, out, column, left):
            given = lax.ppermute(jnp.stack(given), axes, cores)
            if picks:
                pairs = [list(zip(a, p)) for a, p in zip(arrays, picks)]
                out = column_blocks(out, left, pairs, column, width, factor)
            return given, out

        def skip(given, arrays, out, column, left):
            return jnp.stack(given), out

        column = cols.pop(0) if groups else None
        return lax.cond(cols[-1][0] >= 0, run, skip, given, arrays, out, column, left)

    start(0)
    swapped, _ = swap(list(own), [], None)
    start(1)
    for i, step in enumerate(STEPS):
        final = i + 1 == len(STEPS)
        if final:
            groups = due(i)
            out = column_blocks(out, left, groups[:1], cols.pop(0), width, factor)
            cols, out = lax.optimization_barrier((cols, out))
        arrived = [pending.pop(name) for name in step]
        if i == 0:
            swapped, arrived, cols = lax.optimization_barrier((swapped, arrived, cols))
            other.update((("S", 0, h), (swapped, h)) for h in range(2))
        else:
            arrived, cols = lax.optimization_barrier((arrived, cols))
        mine.update(zip(step, arrived))
        if final:
            for name, a in zip(step, arrived):
                other[name] = (lax.ppermute(a, axes, cores), None)
            out = column_blocks(out, left, groups[1:], cols.pop(0), width, factor)
            break
        inside = i in CALLS and out is not None
        swapped, new = swap(arrived, due(i) if inside else [], out if inside else None)
        if inside:
            out = new
        other.update((name, (swapped, j)) for j, name in enumerate(step))
        if i in CALLS and not inside:
            if left is None:
                parts = [p for h in range(2) for p in parts_of(("S", 0, h), ("Y", 0, h))]
                left = left_rows(tok, parts, strip)
            out = column_blocks(out, left, due(i), cols.pop(0), width, factor)
        names = []
        if i + 2 < len(STEPS):
            names = sorted({source(link, name) for link, name in enumerate(STEPS[i + 2])})
        held = ([mine[n] for n in names], swapped, cols, out)
        held, swapped, cols, out = lax.optimization_barrier(held)
        mine.update(zip(names, held))
        other.update((name, (swapped, j)) for j, name in enumerate(step))
        if i + 2 < len(STEPS):
            start(i + 2)
    return column_blocks(out, left, due(len(STEPS)), cols.pop(0), width, factor)


def local(acts):
    if lax.axis_size("blk") == 8 and lax.axis_size("tok") == 4 and acts.shape[2] == 14 * LANES:
        return meshed(acts)
    return gathered(acts)


def solution(mesh):
    return jax.shard_map(
        local,
        mesh=mesh,
        in_specs=(P("tok", None, "blk"),),
        out_specs=P(None, ("blk", "tok"), None),
        check_vma=False,
    )
```

```python
import functools

import jax
import jax.numpy as jnp
from jax import lax
from jax.experimental import pallas as pl
from jax.experimental.pallas import tpu as pltpu
from jax.sharding import PartitionSpec as P

LANES = 128
KSCALE = 1
CALLS = (2, 3, 4, 5, 6, 7, 8, 9, 10)
VMEM = 56 * 2**20


def picked(ref, at):
    return ref if at is None else ref.at[at]


def left_kernel(count, picks, tok_ref, *refs):
    parts, out_ref, held, sems = refs[: 2 * count], refs[-3], refs[-2], refs[-1]
    strip = out_ref.shape[1]
    window = held.shape[2]
    first = tok_ref[0] * strip
    base = pl.multiple_of(first // LANES * LANES, LANES)
    copies = []
    for h in range(2):
        at = 0
        for i, ref in enumerate(parts[h * count : (h + 1) * count]):
            depth = ref.shape[-2]
            copies.append(
                pltpu.make_async_copy(
                    picked(ref, picks[h * count + i]).at[:, pl.ds(base, window)], held.at[h, at : at + depth], sems.at[h, i]
                )
            )
            at += depth
    for copy in copies:
        copy.start()
    row = lax.broadcasted_iota(jnp.int32, (strip, window), 0)
    col = lax.broadcasted_iota(jnp.int32, (strip, window), 1)
    pick = jnp.where(col == row + (first - base), 1.0, 0.0).astype(jnp.bfloat16)
    for copy in copies:
        copy.wait()
    for h in range(2):
        part = lax.dot_general(
            pick, held[h], (((1,), (1,)), ((), ())), preferred_element_type=jnp.float32
        )
        out_ref[h] = part.astype(out_ref.dtype)


def left_rows(tok, parts, strip):
    picks = [p[1] for p in parts]
    parts = [p[0] for p in parts]
    depth = sum(p.shape[-2] for p in parts) // 2
    shape = (2, strip, depth)
    window = (strip + LANES // 2 + LANES - 1) // LANES * LANES
    return pl.pallas_call(
        functools.partial(left_kernel, len(parts) // 2, picks),
        out_shape=jax.ShapeDtypeStruct(shape, jnp.bfloat16),
        in_specs=[pl.BlockSpec(memory_space=pltpu.SMEM)]
        + [pl.BlockSpec(memory_space=pl.ANY)] * len(parts),
        out_specs=pl.BlockSpec(memory_space=pltpu.VMEM),
        scratch_shapes=[
            pltpu.VMEM((2, depth, window), jnp.bfloat16),
            pltpu.SemaphoreType.DMA((2, len(parts) // 2)),
        ],
        compiler_params=pltpu.CompilerParams(vmem_limit_bytes=VMEM),
        cost_estimate=pl.CostEstimate(
            flops=2 * 2 * strip * depth * window,
            bytes_accessed=2 * 2 * depth * (window + strip),
            transcendentals=0,
        ),
    )(tok[None], *parts)


def column_kernel(factor, parts, picks, cols_ref, left_ref, *refs):
    blocks = len(parts)
    count = sum(len(p) for p in parts)
    rights, out_ref, held, sems = refs[:count], refs[-3], refs[-2], refs[-1]
    block, half = pl.program_id(0), pl.program_id(1)
    last = pl.num_programs(1) - 1

    def copies(b):
        first = sum(len(p) for p in parts[:b])
        at, found = 0, []
        for i, depth in enumerate(parts[b]):
            found.append(
                pltpu.make_async_copy(
                    picked(rights[first + i], picks[b][i]),
                    held.at[b % 2, at : at + depth],
                    sems.at[b % 2, i],
                )
            )
            at += depth
        return found

    @pl.when((block == 0) & (half == 0))
    def _():
        for b in range(min(2, blocks)):
            for copy in copies(b):
                copy.start()

    for b in range(blocks):

        @pl.when((block == b) & (half == 0))
        def _(b=b):
            for copy in copies(b):
                copy.wait()

    part = jnp.dot(left_ref[...], held[block % 2], preferred_element_type=jnp.float32)
    out_ref[...] = (part * factor).astype(out_ref.dtype)
    for b in range(blocks - 2):

        @pl.when((block == b) & (half == last))
        def _(b=b):
            for copy in copies(b + 2):
                copy.start()


def column_blocks(out, left, groups, cols, width, factor):
    block = groups[0][0][0].shape[-1]
    halves, strip, depth = left.shape
    parts = [[a.shape[-2] for a, _ in g] for g in groups]
    picks = [[at for _, at in g] for g in groups]
    anywhere = pl.BlockSpec(memory_space=pl.ANY)
    operands = [cols, left] + [a for g in groups for a, _ in g]
    in_specs = [pl.BlockSpec((None, strip, depth), lambda b, i, c: (i, 0, 0))]
    in_specs += [anywhere] * (len(operands) - 2)
    aliases = {}
    if out is not None:
        in_specs.append(anywhere)
        aliases = {len(operands): 0}
        operands.append(out)
    return pl.pallas_call(
        functools.partial(column_kernel, factor, parts, picks),
        out_shape=jax.ShapeDtypeStruct((2, strip, width), jnp.bfloat16),
        grid_spec=pltpu.PrefetchScalarGridSpec(
            num_scalar_prefetch=1,
            grid=(len(groups), halves),
            in_specs=in_specs,
            out_specs=pl.BlockSpec((None, strip, block), lambda b, i, c: (i, 0, c[b])),
            scratch_shapes=[
                pltpu.VMEM((min(2, len(groups)), depth, block), jnp.bfloat16),
                pltpu.SemaphoreType.DMA((2, max(len(p) for p in parts))),
            ],
        ),
        input_output_aliases=aliases,
        compiler_params=pltpu.CompilerParams(vmem_limit_bytes=VMEM),
        cost_estimate=pl.CostEstimate(
            flops=int(KSCALE * 2 * 2 * strip * depth * block * len(groups)),
            bytes_accessed=2 * (depth * (block + 2 * strip) + 2 * strip * block) * len(groups),
            transcendentals=0,
        ),
    )(*operands)


def gathered(acts):
    nblk, ntok = lax.axis_size("blk"), lax.axis_size("tok")
    tok_rows, _, rows = acts.shape
    strip = rows // ntok
    tok = lax.axis_index("tok")
    halves = jnp.swapaxes(acts, 0, 1)
    group = lax.all_gather(halves, "tok", axis=0)
    left = lax.dynamic_slice_in_dim(group, tok * strip, strip, 3)
    whole = lax.all_gather(group, "blk", axis=0)
    order = jnp.concatenate([whole[:, :, 0], whole[::-1, :, 1]], axis=0)
    product = jnp.einsum("thks,ctkr->hscr", left, order, preferred_element_type=jnp.float32)
    scaled = (product * (2.0 / (tok_rows * ntok))).astype(jnp.bfloat16)
    return scaled.reshape(2, strip, 2 * nblk * rows)


STEPS = [
    (("S", 1, 0), ("X", 0, 1), ("Y", 0, 0)),
    (("S", 1, 1), ("X", 0, 0), ("Y", 0, 1)),
    (("S", 2, 0), ("D", 0, 0), ("D", 0, 1)),
    (("S", 2, 1), ("X", 1, 0), ("Y", 1, 0)),
    (("S", 3, 0), ("X", 1, 1), ("Y", 1, 1)),
    (("S", 3, 1), ("X", 2, 0), ("Y", 2, 0)),
    (("D", 1, 0), ("X", 2, 1), ("Y", 2, 1)),
    (("D", 1, 1), ("X", 3, 1), ("Y", 3, 0)),
    (("D", 2, 0), ("X", 3, 0), ("Y", 3, 1)),
    (("D", 2, 1), ("D", 3, 0), ("D", 3, 1)),
]


def source(link, name):
    place, k, h = name
    if link == 0:
        return place, k - 1, h
    if place == "D":
        return ("Y" if link == 1 else "X"), k, h
    return "S", k, h


def meshed(acts):
    nblk, ntok = lax.axis_size("blk"), lax.axis_size("tok")
    nz = nblk // 2
    tok_rows, _, rows = acts.shape
    strip = rows // ntok
    width = 2 * nblk * rows
    factor = 2.0 / (tok_rows * ntok)
    axes = ("blk", "tok")
    places = [
        (z, x, y, c)
        for z in range(nz)
        for x in range(2)
        for y in range(2)
        for c in range(2)
    ]

    def at(z, x, y, c):
        return ((z * 2 + x) * 2 + y) * 2 + c

    links = [
        [(at(z, x, y, c), at((z + 1) % nz, x, y, c)) for z, x, y, c in places],
        [(at(z, x, y, c), at(z, 1 - x, y, c)) for z, x, y, c in places],
        [(at(z, x, y, c), at(z, x, 1 - y, c)) for z, x, y, c in places],
    ]
    cores = [(at(z, x, y, c), at(z, x, y, 1 - c)) for z, x, y, c in places]

    blk, tok = lax.axis_index("blk"), lax.axis_index("tok")
    z, x = blk // 2, blk % 2
    cols = []
    for k in range(nz):
        zk = (z - k) % nz
        for xk in (x, 1 - x):
            cols += [2 * zk + xk, 2 * nblk - 1 - (2 * zk + xk)]
    cols = [c.astype(jnp.int32) for c in cols]

    own = lax.optimization_barrier((acts[:, 0, :], acts[:, 1, :]))
    mine = {("S", 0, 0): own[0], ("S", 0, 1): own[1]}
    other = {}
    ready = {("S", 0, 0): 0, ("S", 0, 1): 0}

    out, left = None, None
    pending = {}
    for i, step in enumerate(STEPS):
        for name in step:
            ready[name] = i + 1
    todo = []
    for k in range(nz):
        for xi, (near, far) in enumerate((("S", "Y"), ("X", "D"))):
            for h in range(2):
                todo.append((max(ready[near, k, h], ready[far, k, h]), (near, k, h), (far, k, h), (2 * k + xi) * 2 + h))
    todo.sort()
    calls, first = [], 0
    for upto in CALLS:
        end = sum(t[0] <= upto for t in todo)
        ends = [first + 1, end] if upto + 1 == len(STEPS) else [end]
        for stop in ends:
            calls.append([t[3] for t in todo[first:stop]])
            first = stop
    cols = [jnp.stack([cols[w] for w in call]) for call in calls]

    def start(i):
        for link, name in enumerate(STEPS[i]):
            pending[name] = lax.ppermute(mine[source(link, name)], axes, links[link])

    def parts_of(near, far):
        return [(mine[near], None), other[near], (mine[far], None), other[far]]

    def due(upto):
        now = [t for t in todo if t[0] <= upto]
        del todo[: len(now)]
        return [parts_of(near, far) for _, near, far, _ in now]

    def swap(given, groups, out, apart=False):
        arrays = [[a for a, _ in g] for g in groups]
        picks = [[at for _, at in g] for g in groups]

        def run(given, arrays, out, column, left):
            given = list(given) if apart else [jnp.stack(given)]
            given = [lax.ppermute(a, axes, cores) for a in given]
            if picks:
                pairs = [list(zip(a, p)) for a, p in zip(arrays, picks)]
                out = column_blocks(out, left, pairs, column, width, factor)
            return given, out

        def skip(given, arrays, out, column, left):
            if picks and out is None:
                out = jnp.zeros((2, strip, width), given[0].dtype)
            return list(given) if apart else [jnp.stack(given)], out

        column = cols.pop(0) if groups else None
        return lax.cond(cols[-1][0] >= 0, run, skip, given, arrays, out, column, left)

    start(0)
    (swapped,), _ = swap(list(own), [], None)
    start(1)
    for i, step in enumerate(STEPS):
        final = i + 1 == len(STEPS)
        if final:
            groups = due(i)
            out = column_blocks(out, left, groups[:1], cols.pop(0), width, factor)
            cols, out = lax.optimization_barrier((cols, out))
        arrived = [pending.pop(name) for name in step]
        if i == 0:
            swapped, arrived, cols = lax.optimization_barrier((swapped, arrived, cols))
            other.update((("S", 0, h), (swapped, h)) for h in range(2))
        else:
            arrived, cols = lax.optimization_barrier((arrived, cols))
        mine.update(zip(step, arrived))
        if final:
            swapped, out = swap(arrived, groups[1:], out, apart=True)
            other.update((name, (a, None)) for name, a in zip(step, swapped))
            break
        if left is None and i in CALLS:
            parts = [p for h in range(2) for p in parts_of(("S", 0, h), ("Y", 0, h))]
            left = left_rows(tok, parts, strip)
        (swapped,), out = swap(arrived, due(i) if i in CALLS else [], out)
        other.update((name, (swapped, j)) for j, name in enumerate(step))
        names = []
        if i + 2 < len(STEPS):
            names = sorted({source(link, name) for link, name in enumerate(STEPS[i + 2])})
        held = ([mine[n] for n in names], swapped, cols, out)
        held, swapped, cols, out = lax.optimization_barrier(held)
        mine.update(zip(names, held))
        other.update((name, (swapped, j)) for j, name in enumerate(step))
        if i + 2 < len(STEPS):
            start(i + 2)
    return column_blocks(out, left, due(len(STEPS)), cols.pop(0), width, factor)


def local(acts):
    if lax.axis_size("blk") == 8 and lax.axis_size("tok") == 4 and acts.shape[2] == 14 * LANES:
        return meshed(acts)
    return gathered(acts)


def solution(mesh):
    return jax.shard_map(
        local,
        mesh=mesh,
        in_specs=(P("tok", None, "blk"),),
        out_specs=P(None, ("blk", "tok"), None),
        check_vma=False,
    )
```

```python
import functools

import jax
import jax.numpy as jnp
from jax import lax
from jax.experimental import pallas as pl
from jax.experimental.pallas import tpu as pltpu
from jax.sharding import PartitionSpec as P

LANES = 128
KSCALE = 1
CALLS = (2, 3, 4, 5, 6, 7, 8, 9, 10)
VMEM = 56 * 2**20


def picked(ref, at):
    return ref if at is None else ref.at[at]


def left_kernel(count, picks, tok_ref, *refs):
    parts, out_ref, held, sems = refs[: 2 * count], refs[-3], refs[-2], refs[-1]
    strip = out_ref.shape[1]
    window = held.shape[2]
    first = tok_ref[0] * strip
    base = pl.multiple_of(first // LANES * LANES, LANES)
    copies = []
    for h in range(2):
        at = 0
        for i, ref in enumerate(parts[h * count : (h + 1) * count]):
            depth = ref.shape[-2]
            copies.append(
                pltpu.make_async_copy(
                    picked(ref, picks[h * count + i]).at[:, pl.ds(base, window)], held.at[h, at : at + depth], sems.at[h, i]
                )
            )
            at += depth
    for copy in copies:
        copy.start()
    row = lax.broadcasted_iota(jnp.int32, (strip, window), 0)
    col = lax.broadcasted_iota(jnp.int32, (strip, window), 1)
    pick = jnp.where(col == row + (first - base), 1.0, 0.0).astype(jnp.bfloat16)
    for copy in copies:
        copy.wait()
    for h in range(2):
        part = lax.dot_general(
            pick, held[h], (((1,), (1,)), ((), ())), preferred_element_type=jnp.float32
        )
        out_ref[h] = part.astype(out_ref.dtype)


def left_rows(tok, parts, strip):
    picks = [p[1] for p in parts]
    parts = [p[0] for p in parts]
    depth = sum(p.shape[-2] for p in parts) // 2
    shape = (2, strip, depth)
    window = (strip + LANES // 2 + LANES - 1) // LANES * LANES
    return pl.pallas_call(
        functools.partial(left_kernel, len(parts) // 2, picks),
        out_shape=jax.ShapeDtypeStruct(shape, jnp.bfloat16),
        in_specs=[pl.BlockSpec(memory_space=pltpu.SMEM)]
        + [pl.BlockSpec(memory_space=pl.ANY)] * len(parts),
        out_specs=pl.BlockSpec(memory_space=pltpu.VMEM),
        scratch_shapes=[
            pltpu.VMEM((2, depth, window), jnp.bfloat16),
            pltpu.SemaphoreType.DMA((2, len(parts) // 2)),
        ],
        compiler_params=pltpu.CompilerParams(vmem_limit_bytes=VMEM),
        cost_estimate=pl.CostEstimate(
            flops=2 * 2 * strip * depth * window,
            bytes_accessed=2 * 2 * depth * (window + strip),
            transcendentals=0,
        ),
    )(tok[None], *parts)


def column_kernel(factor, parts, picks, cols_ref, left_ref, *refs):
    blocks = len(parts)
    count = sum(len(p) for p in parts)
    rights, out_ref, held, sems = refs[:count], refs[-3], refs[-2], refs[-1]
    block, half = pl.program_id(0), pl.program_id(1)
    last = pl.num_programs(1) - 1

    def copies(b):
        first = sum(len(p) for p in parts[:b])
        at, found = 0, []
        for i, depth in enumerate(parts[b]):
            found.append(
                pltpu.make_async_copy(
                    picked(rights[first + i], picks[b][i]),
                    held.at[b % 2, at : at + depth],
                    sems.at[b % 2, i],
                )
            )
            at += depth
        return found

    @pl.when((block == 0) & (half == 0))
    def _():
        for b in range(min(2, blocks)):
            for copy in copies(b):
                copy.start()

    for b in range(blocks):

        @pl.when((block == b) & (half == 0))
        def _(b=b):
            for copy in copies(b):
                copy.wait()

    part = jnp.dot(left_ref[...], held[block % 2], preferred_element_type=jnp.float32)
    out_ref[...] = (part * factor).astype(out_ref.dtype)
    for b in range(blocks - 2):

        @pl.when((block == b) & (half == last))
        def _(b=b):
            for copy in copies(b + 2):
                copy.start()


def column_blocks(out, left, groups, cols, width, factor):
    block = groups[0][0][0].shape[-1]
    halves, strip, depth = left.shape
    parts = [[a.shape[-2] for a, _ in g] for g in groups]
    picks = [[at for _, at in g] for g in groups]
    anywhere = pl.BlockSpec(memory_space=pl.ANY)
    operands = [cols, left] + [a for g in groups for a, _ in g]
    in_specs = [pl.BlockSpec((None, strip, depth), lambda b, i, c: (i, 0, 0))]
    in_specs += [anywhere] * (len(operands) - 2)
    aliases = {}
    if out is not None:
        in_specs.append(anywhere)
        aliases = {len(operands): 0}
        operands.append(out)
    return pl.pallas_call(
        functools.partial(column_kernel, factor, parts, picks),
        out_shape=jax.ShapeDtypeStruct((2, strip, width), jnp.bfloat16),
        grid_spec=pltpu.PrefetchScalarGridSpec(
            num_scalar_prefetch=1,
            grid=(len(groups), halves),
            in_specs=in_specs,
            out_specs=pl.BlockSpec((None, strip, block), lambda b, i, c: (i, 0, c[b])),
            scratch_shapes=[
                pltpu.VMEM((min(2, len(groups)), depth, block), jnp.bfloat16),
                pltpu.SemaphoreType.DMA((2, max(len(p) for p in parts))),
            ],
        ),
        input_output_aliases=aliases,
        compiler_params=pltpu.CompilerParams(vmem_limit_bytes=VMEM),
        cost_estimate=pl.CostEstimate(
            flops=int(KSCALE * 2 * 2 * strip * depth * block * len(groups)),
            bytes_accessed=2 * (depth * (block + 2 * strip) + 2 * strip * block) * len(groups),
            transcendentals=0,
        ),
    )(*operands)


def gathered(acts):
    nblk, ntok = lax.axis_size("blk"), lax.axis_size("tok")
    tok_rows, _, rows = acts.shape
    strip = rows // ntok
    tok = lax.axis_index("tok")
    halves = jnp.swapaxes(acts, 0, 1)
    group = lax.all_gather(halves, "tok", axis=0)
    left = lax.dynamic_slice_in_dim(group, tok * strip, strip, 3)
    whole = lax.all_gather(group, "blk", axis=0)
    order = jnp.concatenate([whole[:, :, 0], whole[::-1, :, 1]], axis=0)
    product = jnp.einsum("thks,ctkr->hscr", left, order, preferred_element_type=jnp.float32)
    scaled = (product * (2.0 / (tok_rows * ntok))).astype(jnp.bfloat16)
    return scaled.reshape(2, strip, 2 * nblk * rows)


STEPS = [
    (("S", 1, 0), ("X", 0, 0), ("Y", 0, 0)),
    (("S", 1, 1), ("X", 0, 1), ("Y", 0, 1)),
    (("S", 2, 0), ("D", 0, 0), ("Y", 1, 0)),
    (("S", 2, 1), ("X", 1, 0), ("D", 0, 1)),
    (("S", 3, 0), ("X", 1, 1), ("Y", 1, 1)),
    (("S", 3, 1), ("X", 2, 0), ("Y", 2, 0)),
    (("D", 1, 0), ("X", 2, 1), ("Y", 2, 1)),
    (("D", 1, 1), ("X", 3, 1), ("Y", 3, 0)),
    (("D", 2, 0), ("X", 3, 0), ("Y", 3, 1)),
    (("D", 2, 1), ("D", 3, 0), ("D", 3, 1)),
]


def source(link, name):
    place, k, h = name
    if link == 0:
        return place, k - 1, h
    if place == "D":
        return ("Y" if link == 1 else "X"), k, h
    return "S", k, h


def meshed(acts):
    nblk, ntok = lax.axis_size("blk"), lax.axis_size("tok")
    nz = nblk // 2
    tok_rows, _, rows = acts.shape
    strip = rows // ntok
    width = 2 * nblk * rows
    factor = 2.0 / (tok_rows * ntok)
    axes = ("blk", "tok")
    places = [
        (z, x, y, c)
        for z in range(nz)
        for x in range(2)
        for y in range(2)
        for c in range(2)
    ]

    def at(z, x, y, c):
        return ((z * 2 + x) * 2 + y) * 2 + c

    links = [
        [(at(z, x, y, c), at((z + 1) % nz, x, y, c)) for z, x, y, c in places],
        [(at(z, x, y, c), at(z, 1 - x, y, c)) for z, x, y, c in places],
        [(at(z, x, y, c), at(z, x, 1 - y, c)) for z, x, y, c in places],
    ]
    cores = [(at(z, x, y, c), at(z, x, y, 1 - c)) for z, x, y, c in places]

    blk, tok = lax.axis_index("blk"), lax.axis_index("tok")
    z, x = blk // 2, blk % 2
    cols = []
    for k in range(nz):
        zk = (z - k) % nz
        for xk in (x, 1 - x):
            cols += [2 * zk + xk, 2 * nblk - 1 - (2 * zk + xk)]
    cols = [c.astype(jnp.int32) for c in cols]

    first, acts = lax.optimization_barrier((acts[:, 0, :], acts))
    own = (first, lax.optimization_barrier(acts[:, 1, :]))
    mine = {("S", 0, 0): own[0], ("S", 0, 1): own[1]}
    other = {}
    ready = {("S", 0, 0): 0, ("S", 0, 1): 0}

    out, left = None, None
    pending = {}
    for i, step in enumerate(STEPS):
        for name in step:
            ready[name] = i + 1
    todo = []
    for k in range(nz):
        for xi, (near, far) in enumerate((("S", "Y"), ("X", "D"))):
            for h in range(2):
                todo.append((max(ready[near, k, h], ready[far, k, h]), (near, k, h), (far, k, h), (2 * k + xi) * 2 + h))
    todo.sort()
    calls, first = [], 0
    for upto in CALLS:
        end = sum(t[0] <= upto for t in todo)
        ends = [first + 1, end] if upto + 1 == len(STEPS) else [end]
        for stop in ends:
            calls.append([t[3] for t in todo[first:stop]])
            first = stop
    cols = [jnp.stack([cols[w] for w in call]) for call in calls]

    def start(i):
        for link, name in enumerate(STEPS[i]):
            pending[name] = lax.ppermute(mine[source(link, name)], axes, links[link])

    def parts_of(near, far):
        return [(mine[near], None), other[near], (mine[far], None), other[far]]

    def due(upto):
        now = [t for t in todo if t[0] <= upto]
        del todo[: len(now)]
        return [parts_of(near, far) for _, near, far, _ in now]

    def swap(given, groups, out, apart=False):
        arrays = [[a for a, _ in g] for g in groups]
        picks = [[at for _, at in g] for g in groups]

        def run(given, arrays, out, column, left):
            given = list(given) if apart else [jnp.stack(given)]
            given = [lax.ppermute(a, axes, cores) for a in given]
            if picks:
                pairs = [list(zip(a, p)) for a, p in zip(arrays, picks)]
                out = column_blocks(out, left, pairs, column, width, factor)
            return given, out

        def skip(given, arrays, out, column, left):
            if picks and out is None:
                out = jnp.zeros((2, strip, width), given[0].dtype)
            return list(given) if apart else [jnp.stack(given)], out

        column = cols.pop(0) if groups else None
        return lax.cond(cols[-1][0] >= 0, run, skip, given, arrays, out, column, left)

    start(0)
    (swapped,), _ = swap(list(own), [], None)
    start(1)
    for i, step in enumerate(STEPS):
        final = i + 1 == len(STEPS)
        if final:
            groups = due(i)
            out = column_blocks(out, left, groups[:1], cols.pop(0), width, factor)
            cols, out = lax.optimization_barrier((cols, out))
        arrived = [pending.pop(name) for name in step]
        if i == 0:
            swapped, arrived, cols = lax.optimization_barrier((swapped, arrived, cols))
            other.update((("S", 0, h), (swapped, h)) for h in range(2))
        else:
            arrived, cols = lax.optimization_barrier((arrived, cols))
        mine.update(zip(step, arrived))
        if final:
            swapped, out = swap(arrived, groups[1:], out, apart=True)
            other.update((name, (a, None)) for name, a in zip(step, swapped))
            break
        if left is None and i in CALLS:
            parts = [p for h in range(2) for p in parts_of(("S", 0, h), ("Y", 0, h))]
            left = left_rows(tok, parts, strip)
        (swapped,), out = swap(arrived, due(i) if i in CALLS else [], out)
        other.update((name, (swapped, j)) for j, name in enumerate(step))
        names = []
        if i + 2 < len(STEPS):
            names = sorted({source(link, name) for link, name in enumerate(STEPS[i + 2])})
        held = ([mine[n] for n in names], swapped, cols, out)
        held, swapped, cols, out = lax.optimization_barrier(held)
        mine.update(zip(names, held))
        other.update((name, (swapped, j)) for j, name in enumerate(step))
        if i + 2 < len(STEPS):
            start(i + 2)
    return column_blocks(out, left, due(len(STEPS)), cols.pop(0), width, factor)


def local(acts):
    if lax.axis_size("blk") == 8 and lax.axis_size("tok") == 4 and acts.shape[2] == 14 * LANES:
        return meshed(acts)
    return gathered(acts)


def solution(mesh):
    return jax.shard_map(
        local,
        mesh=mesh,
        in_specs=(P("tok", None, "blk"),),
        out_specs=P(None, ("blk", "tok"), None),
        check_vma=False,
    )
```
